256 devices in a mesh: replica: 32 (over x_hi, z, core), tensor: 8 (over x_lo, y).
Axes of the slice: x: 4 (x_hi: 2, x_lo: 2; x = x_hi * 2 + x_lo), y: 4, z: 8, core: 2. Of those that a mesh axis runs over, the one named last changes fastest.
Arguments:
- hidden: bfloat16 [32768, 9728], P('replica', 'tensor'), may hold values from -6 to 6
- out_grad: bfloat16 [32768, 1792], P('replica', 'tensor'), may hold values from -0.26367188 to 0.26367188
- token_mask: int32 [32768], P('replica'), may hold values 0 or 1
- momentum: bfloat16 [32, 9728, 1792], P('replica', 'tensor'), may hold values from -6 to 6
Outputs:
- momentum_out: bfloat16 [32, 9728, 1792], P('replica', 'tensor')
- band_update: bfloat16 [9728, 1792], P('tensor')
The draws below stay inside these ranges and needn't reach their ends.
All inputs are finite; a program needn't handle non-finite values. No bound on the sum of `token_mask` on one device may be relied on, other than what follows from the above.
Results may differ from the reference program's by a relative error of at most 0.001.
Values may be sent and summed in bfloat16 or wider, within the bound.
No kernel may reach another device: no remote copies, remote signals or barrier semaphores. Data moves between devices by JAX's collectives and lax.ppermute only.
A program may use at most 128 MiB of HBM per device.

```python
import jax
import jax.numpy as jnp
from jax import lax

DW = 1792
FFW = 9728
TILE = 64
BAND = 8
TOK = 1024
TOKENS = 32768
N_REPLICA = 32


def place_ends(values, rng, smallest, largest):
    spot = [jax.random.randint(jax.random.fold_in(rng, axis), (), 0, length) for axis, length in enumerate(values.shape)]
    main_axis = values.shape.index(max(values.shape))
    next_to = spot[:main_axis] + [(spot[main_axis] + 1) % values.shape[main_axis]] + spot[main_axis + 1:]
    return values.at[tuple(spot)].set(smallest).at[tuple(next_to)].set(largest)


def block_levels(own_key, shape, pieces, smallest, high):
    level = 1.0
    for axis_at, parts in pieces:
        draws = jax.random.uniform(jax.random.fold_in(jax.random.fold_in(own_key, 6), axis_at), (parts,), jnp.float32, smallest / len(pieces), high / len(pieces))
        level = level * jnp.repeat(jnp.exp(draws), shape[axis_at] // parts).reshape((-1,) + (1,) * (len(shape) - 1 - axis_at))
    return level


def gaussian(key, extent, width, most, split=(), held_as=jnp.bfloat16):
    entries = jax.random.normal(key, extent, jnp.float32) * width
    if len(split) > 0:
        entries = block_levels(key, extent, split, -0.22, 0.18) * entries
    return jnp.clip(entries, min=-most, max=most).astype(held_as)


def setup_inputs(seed: int = 0) -> dict:
    splits = jax.random.split(jax.random.key(seed), 5)
    hidden = gaussian(splits[0], (TOKENS, FFW), 1.0, 6.0, ((0, 32), (1, 8)))
    out_grad = gaussian(splits[1], (TOKENS, DW), ((2.0 / TOK) ** 0.5), 0.26367188, ((0, 32), (1, 8)))
    token_mask = place_ends((jax.random.randint(splits[2], (TOKENS,), 0, 2) < 1).astype(jnp.int32), jax.random.fold_in(splits[2], 1), 0, 1)
    momentum = gaussian(splits[3], (N_REPLICA, FFW, DW), 1.0, 6.0, ((0, 32), (1, 8)))
    return dict(hidden=hidden, out_grad=out_grad, token_mask=token_mask, momentum=momentum)


decay_rate = 0.9

def make_basis():
    freqs = jnp.arange(BAND, dtype=jnp.float32)
    cells = jnp.arange(TILE, dtype=jnp.float32)
    scales = jnp.where(freqs == 0, jnp.sqrt(1.0 / TILE), jnp.sqrt(2.0 / TILE)).astype(jnp.float32)
    return scales[:, None] * jnp.cos(jnp.pi * (2.0 * cells[None, :] + 1.0) * freqs[:, None] / (2.0 * TILE))

def band_of(source, dct_basis):
    row_count, col_count = source.shape
    tiled = source.reshape(row_count // TILE, TILE, col_count)
    row_pass = jnp.einsum('ai,xiz->xaz', dct_basis, tiled, precision=lax.Precision.HIGHEST)
    row_pass = row_pass.reshape(row_count // TILE, BAND, col_count // TILE, TILE)
    return jnp.einsum('xayj,bj->xayb', row_pass, dct_basis, precision=lax.Precision.HIGHEST)

def expand(band_coeffs, dct_basis):
    row_tiles, _, col_tiles, _ = band_coeffs.shape
    col_pass = jnp.einsum('xayb,bj->xayj', band_coeffs, dct_basis, precision=lax.Precision.HIGHEST)
    col_pass = col_pass.reshape(row_tiles, BAND, col_tiles * TILE)
    full = jnp.einsum('ai,xaz->xiz', dct_basis, col_pass, precision=lax.Precision.HIGHEST)
    return full.reshape(row_tiles * TILE, col_tiles * TILE)

def reference(hidden, out_grad, token_mask, momentum):
    dct_basis = make_basis()
    chosen = token_mask[:, None] == 1
    weighted = jnp.where(chosen, out_grad, jnp.zeros_like(out_grad))
    hid_rows = hidden.reshape(N_REPLICA, TOK, FFW)
    cot_rows = weighted.reshape(N_REPLICA, TOK, DW)

    def per_replica(members):
        hid_part, cot_part, mom_part = members
        grad = jnp.dot(hid_part.T, cot_part, preferred_element_type=jnp.float32)
        accumulated = decay_rate * mom_part.astype(jnp.float32) + grad
        band_coeffs = band_of(accumulated, dct_basis)
        kept = (accumulated - expand(band_coeffs, dct_basis)).astype(jnp.bfloat16)
        return (kept, band_coeffs)
    momentum_out, band_coeffs = lax.map(per_replica, (hid_rows, cot_rows, momentum))
    band_total = lax.optimization_barrier(jnp.sum(band_coeffs, axis=0))
    band_update = expand(band_total, dct_basis).astype(jnp.bfloat16)
    return (momentum_out, band_update)
```

```python
import functools

import jax
import jax.numpy as jnp
import ml_dtypes
import numpy as np
from jax import lax
from jax.experimental import pallas as pl
from jax.experimental.pallas import tpu as pltpu
from jax.sharding import PartitionSpec as P

TILE, BAND = 64, 8
DECAY = 0.9
TOK, DW = 1024, 1792
ROWS, COLS = 1216, 224
CHUNK = 256
NB = DW // CHUNK
NA = -(-ROWS // CHUNK)
BROWS = NA * 32
BCOLS = DW // TILE * BAND
LIVE = 640
FLAG_ROW = BROWS - 1
F32, BF16 = jnp.float32, jnp.bfloat16
MIB = 1 << 20


def _basis():
    k = np.arange(BAND)[:, None]
    n = np.arange(TILE)[None]
    scale = np.where(k == 0, np.sqrt(1.0 / TILE), np.sqrt(2.0 / TILE))
    return (scale * np.cos(np.pi * (2 * n + 1) * k / (2 * TILE))).astype(np.float32)


def _split(a):
    hi = a.astype(ml_dtypes.bfloat16)
    lo = (a - hi.astype(np.float32)).astype(ml_dtypes.bfloat16)
    return hi, lo


def _constants():
    d = _basis()
    block = np.kron(np.eye(4, dtype=np.float32), d)
    hi, lo = _split(block)
    rows_down = np.concatenate([hi, lo], 0)
    rows_up = np.concatenate([hi, hi, lo, lo], 0).T.copy()
    full_hi, full_lo = _split(np.kron(np.eye(DW // TILE, dtype=np.float32), d))
    seven = np.kron(np.eye(7, dtype=np.float32), d)
    local = []
    for odd in range(2):
        part = seven[24 * odd : 24 * odd + 32, COLS * odd : COLS * odd + COLS]
        local.append(np.concatenate(_split(part), 0))
    return dict(
        rows_down=rows_down,
        rows_up=rows_up,
        full_hi=full_hi,
        full_lo=full_lo,
        local=np.stack(local),
    )


CONST = _constants()


def _dot(a, b, ca=1, cb=0):
    return lax.dot_general(a, b, (((ca,), (cb,)), ((), ())), preferred_element_type=F32)


def _halves(x):
    hi = x.astype(BF16)
    return hi, (x - hi.astype(F32)).astype(BF16)


def _place_live(mask, live):
    ones = (mask == 1).astype(F32)
    at = lax.broadcasted_iota(jnp.int32, (128, 128), 0)
    to = lax.broadcasted_iota(jnp.int32, (128, 128), 1)
    upto = _dot(ones.astype(BF16), (at <= to).astype(BF16))
    slot = lax.broadcasted_iota(jnp.int32, (live, 128), 0).astype(F32)
    before = jnp.zeros((1, 1), F32)
    parts = []
    for s in range(TOK // 128):
        place = upto[s : s + 1, :] + before - 1.0
        place = jnp.where(ones[s : s + 1, :] > 0.5, place, -1.0)
        parts.append(jnp.where(slot == place, 1.0, 0.0).astype(BF16))
        before = before + upto[s : s + 1, 127:128]
    return jnp.concatenate(parts, 1), before


def _expand_setup(band, full_hi, full_lo, stack):
    b_hi, b_lo = _halves(band)
    wide = _dot(b_hi, full_hi[...]) + _dot(b_lo, full_hi[...]) + _dot(b_hi, full_lo[...])
    hi, lo = _halves(wide)
    for a in range(NA):
        for q, part in enumerate((hi, lo, hi, lo)):
            stack[a, 32 * q : 32 * q + 32, :] = part[32 * a : 32 * a + 32, :]


def _weights_kernel(live, parity, mask, cot, local, out_w, out_p, out_n):
    onehot, count = _place_live(mask[...], live)
    picked = _dot(cot[...], onehot, 0, 1).astype(BF16)
    out_w[...] = picked
    both = _dot(local[parity[0]], picked)
    out_p[...] = both[:32] + both[32:]
    out_n[...] = jnp.broadcast_to(count, (8, 128))


def _hidden_kernel(live, mask, hid, rows_down, out_h, out_p):
    onehot, _ = _place_live(mask[...], live)
    for a in range(NA):
        n = min(CHUNK, ROWS - a * CHUNK)
        picked = _dot(hid[:, a * CHUNK : a * CHUNK + n], onehot, 0, 1).astype(BF16)
        out_h[a * CHUNK : a * CHUNK + n, :] = picked
        both = _dot(rows_down[:, :n], picked)
        out_p[32 * a : 32 * a + 32, :] = both[:32] + both[32:]


def _momentum_band_kernel(mom, full_hi, full_lo, rows_down, out):
    down = rows_down[...]
    for a in range(NA):
        n = min(CHUNK, ROWS - a * CHUNK)
        part = mom[a * CHUNK : a * CHUNK + n, :]
        cols = _dot(part, full_hi[...], 1, 1) + _dot(part, full_lo[...], 1, 1)
        hi, lo = _halves(cols)
        both = _dot(down[:, :n], hi)
        out[32 * a : 32 * a + 32, :] = both[:32] + both[32:] + _dot(down[:32, :n], lo)


def _band_kernel(live, places, hid_p, mom_band, count, *refs):
    shards, out, cot_p = refs[:8], refs[8], refs[9]
    cot_p[...] = jnp.zeros_like(cot_p)
    for s, shard in enumerate(shards):
        at = pl.ds(pl.multiple_of(places[s], 8), 32)
        cot_p[at, :] += shard[...]
    h_hi, h_lo = _halves(hid_p[...])
    w_hi, w_lo = _halves(cot_p[...])
    grad = _dot(h_hi, w_hi, 1, 1) + _dot(h_lo, w_hi, 1, 1) + _dot(h_hi, w_lo, 1, 1)
    band = DECAY * mom_band[...] + grad
    row = lax.broadcasted_iota(jnp.int32, band.shape, 0)
    over = jnp.where(count[0:1, 0:1] > live + 0.5, 1.0, 0.0)
    out[...] = jnp.where(row == FLAG_ROW, over, band)


def _momentum_kernel(live, places, band, full_hi, full_lo, rows_up, mom, hid, *refs):
    shards, out, cot, stack, sems = refs[:8], refs[8], refs[9], refs[10], refs[11]

    @pl.when(pl.program_id(0) == 0)
    def _():
        copies = []
        for s, shard in enumerate(shards):
            at = pl.ds(pl.multiple_of(places[s], 16), COLS)
            copies.append(pltpu.make_async_copy(shard, cot.at[at, :], sems.at[s]))
        for c in copies:
            c.start()
        _expand_setup(band[...], full_hi, full_lo, stack)
        for c in copies:
            c.wait()

    grad = _dot(hid[...], cot[...], 1, 1)
    kept = grad - _dot(rows_up[...], stack[pl.program_id(0)])
    out[...] = (DECAY * mom[...].astype(F32) + kept).astype(BF16)


def _update_kernel(band, full_hi, full_lo, rows_up, out, stack):
    @pl.when(pl.program_id(0) == 0)
    def _():
        _expand_setup(band[...], full_hi, full_lo, stack)

    out[...] = _dot(rows_up[...], stack[pl.program_id(0)]).astype(BF16)


VM = pl.BlockSpec(memory_space=pltpu.VMEM)
SM = pl.BlockSpec(memory_space=pltpu.SMEM)
HB = pl.BlockSpec(memory_space=pl.ANY)


def _cost(flops, size):
    return pl.CostEstimate(flops=int(flops), bytes_accessed=int(size), transcendentals=0)


def _struct(shape, dtype):
    return jax.ShapeDtypeStruct(shape, dtype)


def _weights(live, parity, mask, cot, local):
    return pl.pallas_call(
        functools.partial(_weights_kernel, live),
        out_shape=(_struct((COLS, live), BF16), _struct((32, live), F32), _struct((8, 128), F32)),
        in_specs=[SM, VM, VM, VM],
        out_specs=(VM, VM, VM),
        compiler_params=pltpu.CompilerParams(vmem_limit_bytes=24 * MIB),
        cost_estimate=_cost(2 * TOK * live * 256, 1 * MIB),
        name="weights",
    )(parity, mask, cot, local)


def _hidden(live, mask, hid, rows_down):
    return pl.pallas_call(
        functools.partial(_hidden_kernel, live),
        out_shape=(_struct((ROWS, live), BF16), _struct((BROWS, live), F32)),
        in_specs=[VM, VM, VM],
        out_specs=(VM, VM),
        compiler_params=pltpu.CompilerParams(vmem_limit_bytes=32 * MIB),
        cost_estimate=_cost(2 * TOK * live * ROWS, 5 * MIB),
        name="hidden",
    )(mask, hid, rows_down)


def _momentum_band(mom, full_hi, full_lo, rows_down):
    return pl.pallas_call(
        _momentum_band_kernel,
        out_shape=_struct((BROWS, BCOLS), F32),
        in_specs=[VM, VM, VM, VM],
        out_specs=VM,
        compiler_params=pltpu.CompilerParams(vmem_limit_bytes=32 * MIB),
        cost_estimate=_cost(4 * ROWS * DW * 256, 6 * MIB),
        name="momentum_band",
    )(mom, full_hi, full_lo, rows_down)


def _band(live, places, hid_p, mom_band, count, shards):
    return pl.pallas_call(
        functools.partial(_band_kernel, live),
        out_shape=_struct((BROWS, BCOLS), F32),
        in_specs=[SM, VM, VM, VM] + [VM] * 8,
        out_specs=VM,
        scratch_shapes=[pltpu.VMEM((BCOLS, live), F32)],
        compiler_params=pltpu.CompilerParams(vmem_limit_bytes=24 * MIB),
        cost_estimate=_cost(6 * BROWS * 256 * live, 2 * MIB),
        name="band",
    )(places, hid_p, mom_band, count, *shards)


def _momentum(live, places, band, full_hi, full_lo, rows_up, mom, hid, shards):
    return pl.pallas_call(
        functools.partial(_momentum_kernel, live),
        out_shape=_struct((ROWS, DW), BF16),
        grid=(NA,),
        in_specs=[SM, VM, VM, VM, VM, pl.BlockSpec((CHUNK, DW), lambda a: (a, 0)), pl.BlockSpec((CHUNK, live), lambda a: (a, 0))]
        + [HB] * 8,
        out_specs=pl.BlockSpec((CHUNK, DW), lambda a: (a, 0)),
        scratch_shapes=[
            pltpu.VMEM((DW, live), BF16),
            pltpu.VMEM((NA, 128, DW), BF16),
            pltpu.SemaphoreType.DMA((8,)),
        ],
        compiler_params=pltpu.CompilerParams(vmem_limit_bytes=40 * MIB, dimension_semantics=("arbitrary",)),
        cost_estimate=_cost(2 * ROWS * DW * (live + 128), 14 * MIB),
        name="momentum",
    )(places, band, full_hi, full_lo, rows_up, mom, hid, *shards)


def _update(band, full_hi, full_lo, rows_up):
    return pl.pallas_call(
        _update_kernel,
        out_shape=_struct((ROWS, DW), BF16),
        grid=(NA,),
        in_specs=[VM, VM, VM, VM],
        out_specs=pl.BlockSpec((CHUNK, DW), lambda a: (a, 0)),
        scratch_shapes=[pltpu.VMEM((NA, 128, DW), BF16)],
        compiler_params=pltpu.CompilerParams(vmem_limit_bytes=24 * MIB, dimension_semantics=("arbitrary",)),
        cost_estimate=_cost(2 * ROWS * DW * 256, 6 * MIB),
        name="update",
    )(band, full_hi, full_lo, rows_up)


def _tensor_shift(a, dx, dy):
    pairs = [(x * 4 + y, (x + dx) % 2 * 4 + (y + dy) % 4) for x in range(2) for y in range(4)]
    return lax.ppermute(a, "tensor", pairs)


def _replica_shift(a, df, dz, dc):
    pairs = [
        (f * 16 + z * 2 + c, (f + df) % 2 * 16 + (z + dz) % 8 * 2 + (c + dc) % 2)
        for f in range(2)
        for z in range(8)
        for c in range(2)
    ]
    return lax.ppermute(a, "replica", pairs)


SHIFTS = ((0, 0), (0, 1), (0, 3), (1, 0), (0, 2), (1, 1), (1, 3), (1, 2))


def _gather_direct(a):
    return [a if s == (0, 0) else _tensor_shift(a, *s) for s in SHIFTS]


def _gather(a):
    up, down = _tensor_shift(a, 0, 1), _tensor_shift(a, 0, 3)
    across = _tensor_shift(a, 1, 0)
    two = _tensor_shift(a, 0, 2)
    return [a, up, down, across, two, _tensor_shift(up, 1, 0), _tensor_shift(down, 1, 0), _tensor_shift(across, 0, 2)]


def _sum_replicas(band):
    core = lax.axis_index("replica") % 2
    half = BROWS // 2
    mine = lax.dynamic_slice(band, (core * half, 0), (half, BCOLS))
    other = lax.dynamic_slice(band, ((1 - core) * half, 0), (half, BCOLS))
    one = mine + _replica_shift(other, 0, 0, 1)
    below, above = _replica_shift(one, 0, 1, 0), _replica_shift(one, 0, 7, 0)
    two, three = one + above, one + below + above
    eight = three + _replica_shift(three, 0, 5, 0) + _replica_shift(two, 0, 3, 0)
    whole = eight + _replica_shift(eight, 1, 0, 0)
    back = _replica_shift(whole, 0, 0, 1)
    first, second = jnp.where(core == 0, whole, back), jnp.where(core == 0, back, whole)
    return jnp.concatenate([first, second], 0)


def _step(live, hidden, out_grad, mask, mom):
    c = {k: jnp.asarray(v) for k, v in CONST.items()}
    index = lax.axis_index("tensor")
    x, y = index // 4, index % 4
    owners = [(x + dx) % 2 * 4 + (y - dy) % 4 for dx, dy in SHIFTS]
    places = jnp.stack([o * COLS for o in owners]).astype(jnp.int32)
    band_places = jnp.stack([o // 2 * 56 + o % 2 * 24 for o in owners]).astype(jnp.int32)
    parity = (index % 2).astype(jnp.int32).reshape(1)

    cot, cot_p, count = _weights(live, parity, mask, out_grad, c["local"])
    cot_ps = _gather_direct(cot_p)
    hid, hid_p = _hidden(live, mask, hidden, c["rows_down"])
    mom_band = _momentum_band(mom, c["full_hi"], c["full_lo"], c["rows_down"])
    band = _band(live, band_places, hid_p, mom_band, count, cot_ps)
    cots = _gather(cot)
    total = _sum_replicas(band)
    momentum_out = _momentum(live, places, band, c["full_hi"], c["full_lo"], c["rows_up"], mom, hid, cots)
    band_update = _update(total, c["full_hi"], c["full_lo"], c["rows_up"])
    return momentum_out, band_update, total[FLAG_ROW, 0]


def shards(hidden, out_grad, token_mask, momentum):
    mask = token_mask.reshape(8, 128)
    mom = momentum[0]
    state = _step(LIVE, hidden, out_grad, mask, mom)
    momentum_out, band_update, _ = lax.while_loop(
        lambda s: s[2] > 0.5,
        lambda s: _step(TOK, hidden, out_grad, mask, mom),
        state,
    )
    return momentum_out[None], band_update


def solution(mesh):
    placed = (P("replica", "tensor"), P("replica", "tensor"), P("replica"), P("replica", "tensor", None))
    return jax.shard_map(
        shards,
        mesh=mesh,
        in_specs=placed,
        out_specs=(P("replica", "tensor", None), P("tensor", None)),
        check_vma=False,
    )
```

```python
import functools

import jax
import jax.numpy as jnp
import ml_dtypes
import numpy as np
from jax import lax
from jax.experimental import pallas as pl
from jax.experimental.pallas import tpu as pltpu
from jax.sharding import PartitionSpec as P

TILE, BAND = 64, 8
DECAY = 0.9
TOK, DW = 1024, 1792
ROWS, COLS = 1216, 224
CHUNK = 256
NB = DW // CHUNK
NA = -(-ROWS // CHUNK)
BROWS = NA * 32
BCOLS = DW // TILE * BAND
LIVE = 640
FLAG_ROW = BROWS - 1
BIG = [slice(0, 512), slice(512, 1024), slice(1024, ROWS)]
SMALL = [slice(a * CHUNK, min(a * CHUNK + CHUNK, ROWS)) for a in range(NA)]
F32, BF16 = jnp.float32, jnp.bfloat16
MIB = 1 << 20
VMEM_MIB = 20


def _basis():
    k = np.arange(BAND)[:, None]
    n = np.arange(TILE)[None]
    scale = np.where(k == 0, np.sqrt(1.0 / TILE), np.sqrt(2.0 / TILE))
    return (scale * np.cos(np.pi * (2 * n + 1) * k / (2 * TILE))).astype(np.float32)


def _split(a):
    hi = a.astype(ml_dtypes.bfloat16)
    lo = (a - hi.astype(np.float32)).astype(ml_dtypes.bfloat16)
    return hi, lo


def _constants():
    d = _basis()
    block = np.kron(np.eye(4, dtype=np.float32), d)
    hi, lo = _split(block)
    rows_down = np.concatenate([hi, lo], 0)
    rows_up = np.concatenate([hi, hi, lo, lo], 0).T.copy()
    cols_down = np.concatenate([np.kron(np.eye(4, dtype=np.float32)[q : q + 1], rows_down.astype(np.float32).T) for q in range(4)], 0)
    merge = np.zeros((512, BCOLS), np.float32)
    for i in range(BCOLS):
        merge[i // 32 * 64 + i % 32, i] = merge[i // 32 * 64 + 32 + i % 32, i] = 1
    seven = np.kron(np.eye(7, dtype=np.float32), d)
    local = []
    for odd in range(2):
        part = seven[24 * odd : 24 * odd + 32, COLS * odd : COLS * odd + COLS]
        local.append(np.concatenate(_split(part), 0))
    return dict(
        rows_down=rows_down,
        rows_up=rows_up,
        cols_down=cols_down.astype(ml_dtypes.bfloat16),
        merge=merge.astype(ml_dtypes.bfloat16),
        local=np.stack(local),
    )


CONST = _constants()


def _dot(a, b, ca=1, cb=0):
    return lax.dot_general(a, b, (((ca,), (cb,)), ((), ())), preferred_element_type=F32)


def _halves(x):
    hi = x.astype(BF16)
    return hi, (x - hi.astype(F32)).astype(BF16)


def _place_live(mask, live):
    ones = (mask == 1).astype(F32)
    at = lax.broadcasted_iota(jnp.int32, (128, 128), 0)
    to = lax.broadcasted_iota(jnp.int32, (128, 128), 1)
    upto = _dot(ones.astype(BF16), (at <= to).astype(BF16))
    slot = lax.broadcasted_iota(jnp.int32, (live, 128), 0).astype(F32)
    before = jnp.zeros((1, 1), F32)
    parts = []
    for s in range(TOK // 128):
        place = upto[s : s + 1, :] + before - 1.0
        place = jnp.where(ones[s : s + 1, :] > 0.5, place, -1.0)
        parts.append(jnp.where(slot == place, 1.0, 0.0).astype(BF16))
        before = before + upto[s : s + 1, 127:128]
    return jnp.concatenate(parts, 1), before


def _expand_setup(band, down, stack):
    b_hi, b_lo = _halves(band)
    for b in range(NB):
        at = slice(32 * b, 32 * b + 32)
        wide = _dot(b_hi[:, at], down[:32]) + _dot(b_lo[:, at], down[:32]) + _dot(b_hi[:, at], down[32:])
        hi, lo = _halves(wide)
        for a in range(NA):
            for q, part in enumerate((hi, lo, hi, lo)):
                stack[a, 32 * q : 32 * q + 32, CHUNK * b : CHUNK * b + CHUNK] = part[32 * a : 32 * a + 32, :]


def _fetch(sems, *pairs):
    copies = [pltpu.make_async_copy(src, dst, sems.at[i]) for i, (src, dst) in enumerate(pairs)]
    for c in copies:
        c.start()
    return copies


def _wait(copies):
    for c in copies:
        c.wait()


def _rows(src, dst, cuts, sems):
    return [pltpu.make_async_copy(src.at[r, :], dst.at[r, :], sems.at[i]) for i, r in enumerate(cuts)]


def _weights_kernel(live, parity, mask, cot, local, out_w, out_p, out_n, mask_v, cot_v, local_v, w_v, p_v, n_v, sems, out_sems):
    copies = _fetch(sems, (mask, mask_v), (cot, cot_v), (local.at[parity[0]], local_v))
    copies[0].wait()
    onehot, count = _place_live(mask_v[...], live)
    _wait(copies[1:])
    picked = _dot(cot_v[...], onehot, 1, 1).astype(BF16)
    both = _dot(local_v[...], picked)
    w_v[...] = picked
    p_v[...] = both[:32] + both[32:]
    n_v[...] = jnp.broadcast_to(count, (8, 128))
    _wait(_fetch(out_sems, (w_v, out_w), (p_v, out_p), (n_v, out_n)))


def _local_kernel(live, mask, cols_down, rows_down, merge, hid, mom, out_h, out_p, out_m, *refs):
    mask_v, cols_v, rows_v, merge_v, hid_v, cols, wide, sems = refs
    copies = _fetch(sems, (mask, mask_v), (rows_down, rows_v), (hid, hid_v), (cols_down, cols_v), (merge, merge_v))
    _wait(copies[:2])
    down = rows_v[...]
    onehot = _place_live(mask_v[...], live)[0]
    copies[2].wait()
    for r in BIG:
        out_h[r, :] = _dot(hid_v[r, :], onehot, 1, 1).astype(BF16)
    for a, r in enumerate(SMALL):
        both = _dot(down[:, : r.stop - r.start], out_h[r, :])
        hi, lo = _halves(both[:32] + both[32:])
        out_p[32 * a : 32 * a + 32, :] = hi
        out_p[BROWS + 32 * a : BROWS + 32 * a + 32, :] = lo
    _wait(copies[3:])
    for r in BIG:
        cols[r, :256] = _dot(mom[r, :1024], cols_v[...])
        cols[r, 256:] = _dot(mom[r, 1024:], cols_v[:768, :])
    for a, r in enumerate(SMALL):
        n = r.stop - r.start
        hi, lo = _halves(cols[r, :])
        both = _dot(down[:, :n], hi)
        wide[32 * a : 32 * a + 32, :] = both[:32] + both[32:] + _dot(down[:32, :n], lo)
    hi, lo = _halves(wide[...])
    out_m[...] = _dot(hi, merge_v[...]) + _dot(lo, merge_v[...])


def _band_kernel(live, places, parities, hid_p, mom_band, count, local, *refs):
    shards, out, own_across, up_down, local_v, cot_p, sems = refs[:9], *refs[9:]
    whole = [up_down.at[0], up_down.at[1], own_across.at[1], own_across.at[0]]
    copies = _fetch(sems, (local, local_v))
    cot_p[...] = jnp.zeros_like(cot_p)
    for s in range(4):
        whole[s][...] = shards[s][...]
    _wait(copies)
    for s in range(8):
        at = pl.ds(pl.multiple_of(places[s], 8), 32)
        if s < 3:
            both = _dot(local_v[parities[s]], shards[s][...])
            cot_p[at, :] += both[:32] + both[32:]
        else:
            cot_p[at, :] += shards[s + 1][...]
    h_hi, h_lo = hid_p[:BROWS, :], hid_p[BROWS:, :]
    w_hi, w_lo = _halves(cot_p[...])
    grad = _dot(h_hi, w_hi, 1, 1) + _dot(h_lo, w_hi, 1, 1) + _dot(h_hi, w_lo, 1, 1)
    band = DECAY * mom_band[...] + grad
    row = lax.broadcasted_iota(jnp.int32, band.shape, 0)
    over = jnp.where(count[0:1, 0:1] > live + 0.5, 1.0, 0.0)
    out[...] = jnp.where(row == FLAG_ROW, over, band)


def _momentum_kernel(live, places, band, rows_down, rows_up, mom, hid, *refs):
    pairs, out, rows_v, up_v, cot, out_v, stack, sems, out_sems = refs[:4], *refs[4:]
    copies = _fetch(sems, (rows_down, rows_v), (rows_up, up_v))
    stores = _rows(out_v, out, SMALL, out_sems)
    for s in range(8):
        cot[pl.ds(pl.multiple_of(places[s], 16), COLS), :] = pairs[s // 2][s % 2]
    _wait(copies)
    _expand_setup(band[...], rows_v[...], stack)
    for a, r in enumerate(SMALL):
        for b in range(NB):
            w = slice(CHUNK * b, CHUNK * b + CHUNK)
            kept = _dot(hid[r, :], cot[w, :], 1, 1) - _dot(up_v[: r.stop - r.start, :], stack[a, :, w])
            out_v[r, w] = (DECAY * mom[r, w].astype(F32) + kept).astype(BF16)
        stores[a].start()
    _wait(stores)


def _update_kernel(core, mine, back, rows_down, rows_up, out, over, rows_v, up_v, out_v, stack, sems, out_sems):
    copies = _fetch(sems, (rows_down, rows_v), (rows_up, up_v))
    stores = _rows(out_v, out, SMALL, out_sems)
    first = core[0] == 0
    band = jnp.concatenate([jnp.where(first, mine[...], back[...]), jnp.where(first, back[...], mine[...])], 0)
    over[0] = jnp.max(band[FLAG_ROW:, :]).astype(jnp.int32)
    _wait(copies)
    _expand_setup(band, rows_v[...], stack)
    for a, r in enumerate(SMALL):
        out_v[r, :] = _dot(up_v[: r.stop - r.start, :], stack[a]).astype(BF16)
        stores[a].start()
    _wait(stores)


SM = pl.BlockSpec(memory_space=pltpu.SMEM)
VM = pl.BlockSpec(memory_space=pltpu.VMEM)
HB = pl.BlockSpec(memory_space=pltpu.HBM)


def _sems(*n):
    return pltpu.SemaphoreType.DMA(n)


def _struct(shape, dtype):
    return jax.ShapeDtypeStruct(shape, dtype)


def _call(kernel, us, ins, outs, scratch, *args, grant=VMEM_MIB):
    name = kernel.func.__name__ if isinstance(kernel, functools.partial) else kernel.__name__
    return pl.pallas_call(
        kernel,
        out_shape=[_struct(*o[1:]) for o in outs],
        in_specs=ins,
        out_specs=[o[0] for o in outs],
        scratch_shapes=scratch,
        compiler_params=pltpu.CompilerParams(vmem_limit_bytes=grant * MIB),
        cost_estimate=pl.CostEstimate(flops=int(us * 1e9), bytes_accessed=int(us * 3.3e6), transcendentals=0),
        name=name.strip("_"),
    )(*args)


V = pltpu.VMEM
MASK = V((8, 128), jnp.int32)
DOWN = V((64, CHUNK), BF16)
UP = V((CHUNK, 128), BF16)
STACK = V((NA, 128, DW), BF16)


def _weights(live, parity, mask, cot, local):
    return _call(
        functools.partial(_weights_kernel, live),
        2.5,
        [SM, HB, HB, HB],
        [(HB, (COLS, live), BF16), (HB, (32, live), F32), (HB, (8, 128), F32)],
        [MASK, V((COLS, TOK), BF16), V((64, COLS), BF16), V((COLS, live), BF16), V((32, live), F32), V((8, 128), F32), _sems(3), _sems(3)],
        parity, mask, cot, local,
    )


def _local(live, mask, cols_down, rows_down, merge, hid, mom):
    return _call(
        functools.partial(_local_kernel, live),
        6,
        [HB, HB, HB, HB, HB, VM],
        [(VM, (ROWS, live), BF16), (VM, (2 * BROWS, live), BF16), (VM, (BROWS, BCOLS), F32)],
        [MASK, V((1024, 256), BF16), DOWN, V((512, BCOLS), BF16), V((ROWS, TOK), BF16),
         V((ROWS, 512), F32), V((BROWS, 512), F32), _sems(5)],
        mask, cols_down, rows_down, merge, hid, mom,
    )


def _band(live, places, parities, hid_p, mom_band, count, local, shards):
    return _call(
        functools.partial(_band_kernel, live),
        3,
        [SM, SM, VM, VM, VM, HB] + [VM] * 9,
        [(VM, (BROWS, BCOLS), F32), (VM, (2, COLS, live), BF16), (VM, (2, COLS, live), BF16)],
        [V((2, 64, COLS), BF16), V((BCOLS, live), F32), _sems(1)],
        places, parities, hid_p, mom_band, count, local, *shards,
    )


def _momentum(live, places, band, rows_down, rows_up, mom, hid, pairs):
    return _call(
        functools.partial(_momentum_kernel, live),
        8,
        [SM, VM, HB, HB] + [VM] * 6,
        [(HB, (ROWS, DW), BF16)],
        [DOWN, UP, V((DW, live), BF16), V((ROWS, DW), BF16), STACK, _sems(2), _sems(NA)],
        places, band, rows_down, rows_up, mom, hid, *pairs,
    )[0]


def _update(core, mine, back, rows_down, rows_up):
    return _call(
        _update_kernel,
        3.5,
        [SM, VM, VM, HB, HB],
        [(HB, (ROWS, DW), BF16), (SM, (1,), jnp.int32)],
        [DOWN, UP, V((ROWS, DW), BF16), STACK, _sems(2), _sems(NA)],
        core, mine, back, rows_down, rows_up,
    )


def _tensor_shift(a, dx, dy):
    pairs = [(x * 4 + y, (x + dx) % 2 * 4 + (y + dy) % 4) for x in range(2) for y in range(4)]
    return lax.ppermute(a, "tensor", pairs)


def _replica_shift(a, df, dz, dc):
    pairs = [
        (f * 16 + z * 2 + c, (f + df) % 2 * 16 + (z + dz) % 8 * 2 + (c + dc) % 2)
        for f in range(2)
        for z in range(8)
        for c in range(2)
    ]
    return lax.ppermute(a, "replica", pairs)


SHIFTS = ((0, 1), (0, 3), (1, 0), (0, 0), (0, 2), (1, 2), (1, 1), (1, 3))


def _sum_planes(band, core):
    half = BROWS // 2
    mine = lax.dynamic_slice(band, (core * half, 0), (half, BCOLS))
    other = lax.dynamic_slice(band, ((1 - core) * half, 0), (half, BCOLS))
    one = mine + _replica_shift(other, 0, 0, 1)
    below, above = _replica_shift(one, 0, 1, 0), _replica_shift(one, 0, 7, 0)
    two, three = one + above, one + below + above
    return three, _replica_shift(three, 0, 5, 0), _replica_shift(two, 0, 3, 0)


def _step(live, hidden, out_grad, mask, mom):
    c = {k: jnp.asarray(v) for k, v in CONST.items()}
    index = lax.axis_index("tensor").astype(jnp.int32)
    core = (lax.axis_index("replica") % 2).astype(jnp.int32)
    x, y = index // 4, index % 4
    owners = [(x + dx) % 2 * 4 + (y - dy) % 4 for dx, dy in SHIFTS]
    places = jnp.stack([owners[s] * COLS for s in (3, 2, 4, 5, 0, 1, 6, 7)])
    band_places = jnp.stack([o // 2 * 56 + o % 2 * 24 for o in owners])

    parities = jnp.stack([o % 2 for o in owners])

    cot, cot_p, count = _weights(live, (index % 2).reshape(1), mask, out_grad, c["local"])
    far_p = [_tensor_shift(cot_p, *s) for s in SHIFTS[4:]]
    near = [_tensor_shift(cot, *s) for s in SHIFTS[:3]]
    hid, hid_p, mom_band = _local(live, mask, c["cols_down"], c["rows_down"], c["merge"], hidden, mom)
    band, own_across, up_down = _band(live, band_places, parities, hid_p, mom_band, count, c["local"], near + [cot, cot_p] + far_p)
    opposite, beside = _tensor_shift(own_across, 0, 2), _tensor_shift(up_down, 1, 0)
    sums = _sum_planes(band, core)
    *sums, opposite, beside = lax.optimization_barrier((*sums, opposite, beside))
    eight = sums[0] + sums[1] + sums[2]
    whole = eight + _replica_shift(eight, 1, 0, 0)
    pairs = [own_across, opposite, up_down, beside]
    momentum_out = _momentum(live, places, band, c["rows_down"], c["rows_up"], mom, hid, pairs)
    whole, momentum_out = lax.optimization_barrier((whole, momentum_out))
    back = _replica_shift(whole, 0, 0, 1)
    band_update, over = _update(core.reshape(1), whole, back, c["rows_down"], c["rows_up"])
    return momentum_out, band_update, over.reshape(())


def shards(hidden, out_grad, token_mask, momentum):
    mask = token_mask.reshape(8, 128)
    hidden, out_grad = hidden.T, out_grad.T
    mom = momentum[0]
    state = _step(LIVE, hidden, out_grad, mask, mom)
    momentum_out, band_update, _ = lax.while_loop(
        lambda s: s[2] > 0,
        lambda s: _step(TOK, hidden, out_grad, jnp.where(s[2] > 0, mask, 0), mom),
        state,
    )
    return momentum_out[None], band_update


def solution(mesh):
    placed = (P("replica", "tensor"), P("replica", "tensor"), P("replica"), P("replica", "tensor", None))
    return jax.shard_map(
        shards,
        mesh=mesh,
        in_specs=placed,
        out_specs=(P("replica", "tensor", None), P("tensor", None)),
        check_vma=False,
    )
```
